32 devices in a mesh: ctx: 8 (over z, x), head: 4 (over y, core).
Axes of the slice: x: 2, y: 2, z: 4, core: 2. Of those that a mesh axis runs over, the one named last changes fastest.
Arguments:
- features: bfloat16 [2048, 16384], P('ctx', 'head'), may hold values from -6 to 6
- log_decay: float32 [256, 2048], P('head', 'ctx'), may hold values from -2 to 0, as said below
- step_size: float32 [256, 2048], P('head', 'ctx'), may hold values from 0.0002 to 0.002
- b_matrix: bfloat16 [2048, 2048], P('ctx', 'head'), may hold values from -6 to 6
- c_matrix: bfloat16 [2048, 2048], P('ctx', 'head'), may hold values from -6 to 6
- skip_gain: float32 [256], P('head'), may hold values from 0.5 to 1.5
Outputs:
- mixed: bfloat16 [2048, 16384], P('ctx', 'head')
The draws below stay inside these ranges and needn't reach their ends.
Inputs may be any that keep to these rules, and one draw needn't show every extreme that they name: `log_decay`: every entry is negative.
All inputs are finite; a program needn't handle non-finite values.
Results may differ from the reference program's by a relative error of at most 0.0013.
Values sent between devices are 32-bit elements; how exact they have to be, the bound alone decides.
A program may use at most 320 MiB of HBM per device.

```python
import math
import jax
import jax.numpy as jnp
from jax import lax

H = 256
P_SIZE = 64
N = 256
G = 8
SPAN = 128
BLK = 128
SEQ = 2048
N_CTX = 8


def draw_log_decay(key, part):
    keys = jax.random.split(key, 7)
    share = 0.5
    picker = jax.random.uniform(keys[0], (H,))
    fast_rate = jnp.exp(jax.random.uniform(keys[1], (H,), jnp.float32, math.log(1.0 / 50.0), math.log(1.0 / 30.0)))
    slow_rate = jnp.exp(jax.random.uniform(keys[2], (H,), jnp.float32, math.log(0.02), math.log(0.3))) / SEQ
    decay_speed = jnp.where(picker < share, fast_rate, slow_rate)
    coarse_estimate = jnp.exp(jax.random.uniform(keys[3], (H, SEQ), jnp.float32, math.log(0.5), math.log(1.5)))
    block_multiplier = jnp.exp(jax.random.uniform(keys[4], (H, SEQ // BLK), jnp.float32, math.log(0.5), math.log(2.0)))
    block_multiplier = jnp.repeat(block_multiplier, BLK, axis=1)
    location_list = jax.random.randint(keys[5], (2,), 0, SEQ)
    stack_height = jax.random.uniform(keys[6], (2,), jnp.float32, 0.22, 0.6)
    token_location = jnp.arange(SEQ)
    spike_level = jnp.sum(jnp.where(token_location[None, :] == location_list[:, None], stack_height[:, None], 0.0), axis=0)
    return -(decay_speed[:, None] * coarse_estimate * block_multiplier + spike_level[None, :])


def levels(key, dims, cuts, low, high):
    gain, own = 1.0, jax.random.fold_in(key, 6)
    for position, shards_of in cuts:
        steps = jnp.exp(jax.random.uniform(jax.random.fold_in(own, position), (shards_of,), jnp.float32, low / len(cuts), high / len(cuts)))
        gain = gain * jnp.repeat(steps, dims[position] // shards_of).reshape([-1 if axis == position else 1 for axis in range(len(dims))])
    return gain


def centred(stream_key, extent, deviation, most, cuts=(), kind=jnp.bfloat16):
    entries = deviation * jax.random.normal(stream_key, extent, jnp.float32)
    if cuts:
        entries = entries * levels(stream_key, extent, cuts, -0.22, 0.18)
    return jnp.clip(entries, -most, most).astype(kind)


def setup_inputs(seed: int = 0) -> dict:
    key_list = jax.random.split(jax.random.key(seed), 7)
    features = centred(key_list[0], (SEQ, H * P_SIZE), 1.0, 6.0, ((0, 8), (1, 4)))
    log_decay = draw_log_decay(jax.random.fold_in(key_list[6], 71), 0)
    step_size = jnp.clip(jnp.exp(math.log(0.002) - 2.3025852 * jax.random.uniform(key_list[2], (H, SEQ), jnp.float32) ** levels(key_list[2], (H, SEQ), ((0, 4), (1, 8)), -0.2, 0.2)), 0.0002, 0.002)
    b_matrix = centred(key_list[3], (SEQ, G * N), 1.0, 6.0, ((0, 8), (1, 4)))
    c_matrix = centred(key_list[4], (SEQ, G * N), 1.0, 6.0, ((0, 8), (1, 4)))
    skip_gain = jnp.clip(0.5 + 1.0 * jax.random.uniform(key_list[5], (H,), jnp.float32) ** levels(key_list[5], (H,), ((0, 4),), -0.2, 0.2), 0.5, 1.5)
    return dict(features=features, log_decay=log_decay, step_size=step_size, b_matrix=b_matrix, c_matrix=c_matrix, skip_gain=skip_gain)


def to_sequence(stored):
    blocks = stored.reshape((N_CTX, 2, BLK) + stored.shape[1:])
    return jnp.concatenate([blocks[:, 0], blocks[::-1, 1]], axis=0).reshape(stored.shape)


def to_stored(ordered):
    blocks = ordered.reshape((2 * N_CTX, BLK) + ordered.shape[1:])
    return jnp.stack([blocks[:N_CTX], blocks[N_CTX:][::-1]], axis=1).reshape(ordered.shape)


def reference(features, log_decay, step_size, b_matrix, c_matrix, skip_gain):
    span_count = SEQ // SPAN
    per_group = H // G
    feat_seq = to_sequence(features).reshape(span_count, SPAN, H, P_SIZE)
    decay_seq = to_sequence(log_decay.T).reshape(span_count, SPAN, H)
    step_seq = to_sequence(step_size.T).reshape(span_count, SPAN, H)
    b_seq = to_sequence(b_matrix).reshape(span_count, SPAN, G, N)
    c_seq = to_sequence(c_matrix).reshape(span_count, SPAN, G, N)
    causal = jnp.arange(SPAN)[:, None] >= jnp.arange(SPAN)[None, :]

    def one_span(state, packed):
        inputs, decay, step_rows, b_rows, c_rows = packed
        cumulative = jnp.cumsum(decay, axis=0)
        b_float = b_rows.astype(jnp.float32)
        c_float = c_rows.astype(jnp.float32)
        scores = jnp.einsum("tgn,sgn->tsg", c_float, b_float)
        scores = jnp.repeat(scores, per_group, axis=2)
        decay_gaps = jnp.where(causal[:, :, None], cumulative[:, None, :] - cumulative[None, :, :], -jnp.inf)
        weights = (scores * jnp.exp(decay_gaps) * step_rows[None, :, :]).astype(jnp.bfloat16)
        weights = lax.optimization_barrier(weights)
        diagonal_part = jnp.einsum("tsh,shp->thp", weights.astype(jnp.float32), inputs.astype(jnp.float32))
        state_bf = lax.optimization_barrier(state.astype(jnp.bfloat16))
        state_grouped = state_bf.astype(jnp.float32).reshape(G, per_group, P_SIZE, N)
        state_part = jnp.einsum("tgn,gqpn->tgqp", c_float, state_grouped).reshape(SPAN, H, P_SIZE)
        state_part = state_part * jnp.exp(cumulative)[:, :, None]
        coeffs = jnp.exp(cumulative[-1:] - cumulative) * step_rows
        weighted = (inputs.astype(jnp.float32) * coeffs[:, :, None]).astype(jnp.bfloat16)
        weighted = lax.optimization_barrier(weighted)
        weighted_grouped = weighted.astype(jnp.float32).reshape(SPAN, G, per_group, P_SIZE)
        span_state = jnp.einsum("sgn,sgqp->gqpn", b_float, weighted_grouped).reshape(H, P_SIZE, N)
        new_state = jnp.exp(cumulative[-1])[:, None, None] * state + span_state
        output = diagonal_part + state_part + skip_gain[None, :, None] * inputs.astype(jnp.float32)
        return new_state, output.astype(jnp.bfloat16)

    start = jnp.zeros((H, P_SIZE, N), jnp.float32)
    final_state, outputs = lax.scan(one_span, start, (feat_seq, decay_seq, step_seq, b_seq, c_seq))
    return to_stored(outputs.reshape(SEQ, H * P_SIZE))
```

```python
import functools

import jax
import jax.numpy as jnp
from jax import lax
from jax.experimental import pallas as pl
from jax.experimental.pallas import tpu as pltpu
from jax.sharding import PartitionSpec as P

N = 256
SPAN = 128
UNIT = 8
MESH = pl.DeviceIdType.MESH
LIMIT = 56 * 1024 * 1024
BF = jnp.bfloat16
F32 = jnp.float32


def scale_kernel(width, x_ref, co_ref, wt_ref):
    for h in range(UNIT):
        cols = slice(h * width, (h + 1) * width)
        wt_ref[:, cols] = (x_ref[:, cols].astype(F32) * co_ref[0, :, h : h + 1]).astype(BF).astype(F32)


def mix_kernel(width, x_ref, ct_ref, cr_ref, st_ref, b_ref, c_ref, skip_ref, sp_ref, o_ref):
    row = lax.broadcasted_iota(jnp.int32, (SPAN, SPAN), 0)
    col = lax.broadcasted_iota(jnp.int32, (SPAN, SPAN), 1)
    causal = row >= col
    for k in range(2):
        toks = slice(k * SPAN, (k + 1) * SPAN)
        scores = lax.dot_general(
            c_ref[toks, :], b_ref[toks, :], (((1,), (1,)), ((), ())), preferred_element_type=F32
        )
        for h in range(UNIT):
            cols = slice(h * width, (h + 1) * width)
            down = ct_ref[0, toks, h : h + 1]
            gaps = jnp.where(causal, down - cr_ref[0, h : h + 1, toks], -jnp.inf)
            weights = (scores * jnp.exp(gaps) * st_ref[0, h : h + 1, toks]).astype(BF)
            x = x_ref[toks, cols]
            part = jnp.dot(weights, x, preferred_element_type=F32)
            part = part + sp_ref[toks, cols] * jnp.exp(down)
            o_ref[toks, cols] = (part + skip_ref[:, cols] * x.astype(F32)).astype(BF)


def chain_kernel(
    n, chunk, glanes, wt, bt, cc, dec, out,
    bt_in, cc_in, dec_in, x_in, b_slot, c_slot, d_slot, states, f_out, f_in, k_out, k_in, y_out,
    small_s, small_r, x_s, x_r, f_s, f_r, k_s, k_r, yf_s, yf_r, yk_s, yk_r,
):
    me = lax.axis_index("ctx")
    level, side = me // 2, lax.rem(me, 2)
    levels = n // 2
    partner = me + 1 - 2 * side
    after, before = lax.rem(me + 2, n), lax.rem(me + n - 2, n)
    half = dec_in.shape[1]
    count = half // chunk
    groups = bt.shape[0] // N
    held = bt_in.shape[0] // N
    mine, other = side * half, (1 - side) * half
    g_mine, g_other = (side * groups) // 2 * N, ((1 - side) * groups) // 2 * N

    barrier = pltpu.get_barrier_semaphore()
    for device in (partner, after, before):
        pl.semaphore_signal(barrier, inc=1, device_id={"ctx": device}, device_id_type=MESH)
    pl.semaphore_wait(barrier, 3)

    def remote(src, dst, send, recv, device):
        return pltpu.make_async_remote_copy(
            src_ref=src, dst_ref=dst, send_sem=send, recv_sem=recv,
            device_id={"ctx": device}, device_id_type=MESH,
        )

    def at(start, length):
        return pl.ds(pl.multiple_of(start, 128), length)

    smalls = [
        remote(bt.at[at(g_other, held * N), :], bt_in, small_s.at[0], small_r.at[0], partner),
        remote(cc.at[:, at(g_other, held * N)], cc_in, small_s.at[1], small_r.at[1], partner),
        remote(dec.at[:, at(other, half)], dec_in, small_s.at[2], small_r.at[2], partner),
    ]

    def x_copy(c):
        return remote(wt.at[:, at(other + c * chunk, chunk)], x_in.at[c], x_s.at[c], x_r.at[c], partner)

    def f_copy(c):
        return remote(f_out.at[c], f_in.at[c], f_s.at[c], f_r.at[c], after)

    def k_copy(c):
        return remote(k_out.at[c], k_in.at[c], k_s.at[c], k_r.at[c], before)

    def y_copy(c, k):
        send, recv = (yf_s, yf_r) if k == 0 else (yk_s, yk_r)
        return remote(
            y_out.at[k, c], out.at[pl.ds(k * SPAN, SPAN), at(mine + c * chunk, chunk)],
            send.at[c], recv.at[c], partner,
        )

    def y_landed(c, k):
        send, recv = (yf_s, yf_r) if k == 0 else (yk_s, yk_r)
        return remote(
            y_out.at[k, c], out.at[pl.ds(k * SPAN, SPAN), at(other + c * chunk, chunk)],
            send.at[c], recv.at[c], partner,
        )

    for copy in smalls:
        copy.start()

    @pl.loop(0, count)
    def _(c):
        x_copy(c).start()

    here = (side, 3 - side)
    there = (1 - side, 2 + side)
    for k in range(2):
        toks = slice(k * SPAN, (k + 1) * SPAN)
        b_slot[here[k]] = bt[at(g_mine, held * N), toks].astype(BF)
        c_slot[here[k]] = cc[toks, at(g_mine, held * N)].astype(BF)
        d_slot[here[k]] = jnp.broadcast_to(dec[k : k + 1, at(mine, half)], (8, half))
    for copy in smalls:
        copy.wait_recv()
    for k in range(2):
        toks = slice(k * SPAN, (k + 1) * SPAN)
        b_slot[there[k]] = bt_in[:, toks].astype(BF)
        c_slot[there[k]] = cc_in[toks, :].astype(BF)
        d_slot[there[k]] = jnp.broadcast_to(dec_in[k : k + 1, :], (8, half))

    def group_rows(c):
        return at((c * chunk) // glanes * N, N)

    def outputs(c, k, slot, entering):
        y = jnp.dot(
            c_slot[slot, :, group_rows(c)], entering.astype(BF), preferred_element_type=F32
        )

        @pl.when(here[k] == slot)
        def _():
            out[pl.ds(k * SPAN, SPAN), at(mine + c * chunk, chunk)] = y

        @pl.when(here[k] != slot)
        def _():
            y_out[k, c] = y

    def advance(c, slot, entering):
        d = d_slot[slot, 0:1, at(c * chunk, chunk)]
        return d * entering + states[c, slot]

    def forward(c):
        x_copy(c).wait_recv()
        for k in range(2):
            toks = slice(k * SPAN, (k + 1) * SPAN)
            states[c, here[k]] = jnp.dot(
                b_slot[here[k], group_rows(c), :], wt[toks, at(mine + c * chunk, chunk)].astype(BF),
                preferred_element_type=F32,
            )
            states[c, there[k]] = jnp.dot(
                b_slot[there[k], group_rows(c), :], x_in[c, toks, :].astype(BF),
                preferred_element_type=F32,
            )

        @pl.when(level == 0)
        def _():
            f_in[c] = jnp.zeros(f_in.shape[1:], F32)

        @pl.when(level > 0)
        def _():
            f_copy(c).wait_recv()

        first = f_in[c]
        second = advance(c, 0, first)
        last = advance(c, 1, second)

        @pl.when(level < levels - 1)
        def _():
            f_out[c] = last
            f_copy(c).start()

        @pl.when(level == levels - 1)
        def _():
            k_in[c] = last

        outputs(c, 0, 0, first)
        outputs(c, 0, 1, second)
        y_copy(c, 0).start()

    def backward(c):
        @pl.when(level < levels - 1)
        def _():
            k_copy(c).wait_recv()

        first = k_in[c]
        second = advance(c, 2, first)

        @pl.when(level > 0)
        def _():
            k_out[c] = advance(c, 3, second)
            k_copy(c).start()

        outputs(c, 1, 2, first)
        outputs(c, 1, 3, second)
        y_copy(c, 1).start()

    lag = 2 * (levels - level) - 1

    @pl.loop(0, count + 2 * levels - 1)
    def _(t):
        @pl.when(t < count)
        def _():
            forward(t)

        @pl.when(jnp.logical_and(t >= lag, t < lag + count))
        def _():
            backward(t - lag)

    for copy in smalls:
        copy.wait_send()

    @pl.loop(0, count)
    def _(c):
        x_copy(c).wait_send()

        @pl.when(level < levels - 1)
        def _():
            f_copy(c).wait_send()

        @pl.when(level > 0)
        def _():
            k_copy(c).wait_send()

        for k in range(2):
            y_copy(c, k).wait_send()
            y_landed(c, k).wait_recv()


def on_device(features, log_decay, step_size, b_matrix, c_matrix, skip_gain):
    heads, rows = log_decay.shape
    lanes = features.shape[1]
    width = lanes // heads
    groups = b_matrix.shape[1] // N
    per_group = heads // groups
    units = heads // UNIT
    n = lax.axis_size("ctx")

    upto = (jnp.arange(SPAN)[:, None] <= jnp.arange(SPAN)[None, :]).astype(F32)
    cumulative = jnp.einsum(
        "hks,st->hkt", log_decay.reshape(heads, 2, SPAN), upto, precision=lax.Precision.HIGHEST
    )
    ends = cumulative[:, :, -1]
    coeffs = jnp.exp(ends[:, :, None] - cumulative).reshape(heads, rows) * step_size
    cumulative = cumulative.reshape(heads, rows)
    cum_rows = cumulative.reshape(units, UNIT, rows)
    step_rows = step_size.reshape(units, UNIT, rows)
    cum_cols = jnp.swapaxes(cum_rows, 1, 2)
    coeff_cols = jnp.swapaxes(coeffs.reshape(units, UNIT, rows), 1, 2)
    skip_row = jnp.repeat(skip_gain, width)[None, :]
    decay = jnp.repeat(jnp.exp(ends).T, width, axis=1)
    decay = jnp.concatenate([decay, jnp.zeros((6, lanes), F32)], axis=0)

    wide = pl.BlockSpec((rows, UNIT * width), lambda j: (0, j))
    tall = pl.BlockSpec((1, rows, UNIT), lambda j: (j, 0, 0))
    flat = pl.BlockSpec((1, UNIT, rows), lambda j: (j, 0, 0))
    grouped = pl.BlockSpec((rows, N), lambda j: (0, j * UNIT // per_group))
    line = pl.BlockSpec((1, UNIT * width), lambda j: (0, j))

    weighted = pl.pallas_call(
        functools.partial(scale_kernel, width),
        grid=(units,),
        out_shape=jax.ShapeDtypeStruct((rows, lanes), F32),
        in_specs=[wide, tall],
        out_specs=wide,
    )(features, coeff_cols)

    half = lanes // 2
    chunk = min(256, half)
    count = half // chunk
    held = max(1, groups // 2)
    vmem = pl.BlockSpec(memory_space=pltpu.VMEM)
    dma = lambda k: pltpu.SemaphoreType.DMA((k,))
    state = pltpu.VMEM((count, N, chunk), F32)
    state_part = pl.pallas_call(
        functools.partial(chain_kernel, n, chunk, per_group * width),
        out_shape=jax.ShapeDtypeStruct((rows, lanes), F32),
        in_specs=[vmem] * 4,
        out_specs=vmem,
        scratch_shapes=[
            pltpu.VMEM((held * N, rows), F32),
            pltpu.VMEM((rows, held * N), F32),
            pltpu.VMEM((8, half), F32),
            pltpu.VMEM((count, rows, chunk), F32),
            pltpu.VMEM((4, held * N, SPAN), BF),
            pltpu.VMEM((4, SPAN, held * N), BF),
            pltpu.VMEM((4, 8, half), F32),
            pltpu.VMEM((count, 4, N, chunk), F32),
            state, state, state, state,
            pltpu.VMEM((2, count, SPAN, chunk), F32),
            dma(3), dma(3),
        ] + [dma(count)] * 10,
        compiler_params=pltpu.CompilerParams(
            collective_id=0, has_side_effects=True, vmem_limit_bytes=LIMIT
        ),
    )(weighted, b_matrix.T.astype(F32), c_matrix.astype(F32), decay)

    return pl.pallas_call(
        functools.partial(mix_kernel, width),
        grid=(units,),
        out_shape=jax.ShapeDtypeStruct((rows, lanes), BF),
        in_specs=[wide, tall, flat, flat, grouped, grouped, line, wide],
        out_specs=wide,
    )(features, cum_cols, cum_rows, step_rows, b_matrix, c_matrix, skip_row, state_part)


def solution(mesh):
    placed = (
        P("ctx", "head"),
        P("head", "ctx"),
        P("head", "ctx"),
        P("ctx", "head"),
        P("ctx", "head"),
        P("head"),
    )
    return jax.shard_map(
        on_device, mesh=mesh, in_specs=placed, out_specs=P("ctx", "head"), check_vma=False
    )
```

```python
import functools

import jax
import jax.numpy as jnp
from jax import lax
from jax.experimental import pallas as pl
from jax.experimental.pallas import tpu as pltpu
from jax.sharding import PartitionSpec as P

N = 256
SPAN = 128
UNIT = 4
REST = 3
MESH = pl.DeviceIdType.MESH
LIMIT = 56 * 1024 * 1024
BF = jnp.bfloat16
F32 = jnp.float32


def spread(values, width):
    rows = values.shape[0]
    return jnp.concatenate(
        [jnp.broadcast_to(values[:, h : h + 1], (rows, width)) for h in range(UNIT)], axis=1
    )


def layer_kernel(
    n, per_group, width, x_ref, cols_ref, rows_ref, step_ref, b_ref, c_ref, skip_ref, o_ref,
    b_out, c_out, d_out, x_out, b_in, c_in, d_in, x_in, b_slot, c_slot, d_slot, scores, acc,
    states, f_out, f_in, k_out, k_in, y_out, y_in,
    small_s, small_r, x_s, x_r, f_s, f_r, k_s, k_r, yf_s, yf_r, yk_s, yk_r,
):
    me = lax.axis_index("ctx")
    level, side = me // 2, lax.rem(me, 2)
    levels = n // 2
    partner = me + 1 - 2 * side
    after, before = lax.rem(me + 2, n), lax.rem(me + n - 2, n)
    chunk = UNIT * width
    count = d_in.shape[1] // chunk
    groups = b_ref.shape[1] // N
    held = b_in.shape[1] // N
    mine, other = side * count, (1 - side) * count
    g_mine, g_other = (side * groups) // 2 * N, ((1 - side) * groups) // 2 * N

    def remote(src, dst, send, recv, device):
        return pltpu.make_async_remote_copy(
            src_ref=src, dst_ref=dst, send_sem=send, recv_sem=recv,
            device_id={"ctx": device}, device_id_type=MESH,
        )

    def at(start, length):
        return pl.ds(pl.multiple_of(start, 128), length)

    def lanes(unit):
        return at(unit * chunk, chunk)

    def toks(k):
        return slice(k * SPAN, (k + 1) * SPAN)

    b_copy = remote(b_out, b_in, small_s.at[0], small_r.at[0], partner)
    c_copy = remote(c_out, c_in, small_s.at[1], small_r.at[1], partner)
    d_copy = remote(d_out, d_in, small_s.at[2], small_r.at[2], partner)

    def x_copy(c):
        return remote(x_out.at[c], x_in.at[c], x_s.at[c], x_r.at[c], partner)

    def f_copy(c):
        return remote(f_out.at[c], f_in.at[c], f_s.at[c], f_r.at[c], after)

    def k_copy(c):
        return remote(k_out.at[c], k_in.at[c], k_s.at[c], k_r.at[c], before)

    def y_copy(c, k):
        send, recv = (yf_s, yf_r) if k == 0 else (yk_s, yk_r)
        return remote(y_out.at[k, c], y_in.at[k, c], send.at[c], recv.at[c], partner)

    def weighted(unit):
        coeffs = spread(cols_ref[unit, :, UNIT : 2 * UNIT], width)
        return (x_ref[:, lanes(unit)].astype(F32) * coeffs).astype(BF)

    def decays(unit):
        ends = [
            jnp.exp(cols_ref[unit, (k + 1) * SPAN - 8 : (k + 1) * SPAN, 0:UNIT])[7:8] for k in range(2)
        ]
        front, back = (jnp.broadcast_to(spread(e, width), (8, chunk)) for e in ends)
        return jnp.where(lax.broadcasted_iota(jnp.int32, (8, chunk), 0) < 4, front, back)

    def send_x(c):
        x_out[c] = weighted(other + c).astype(F32)
        x_copy(c).start()

    barrier = pltpu.get_barrier_semaphore()
    for device in (partner, after, before):
        pl.semaphore_signal(barrier, inc=1, device_id={"ctx": device}, device_id_type=MESH)
    b_out[...] = b_ref[:, at(g_other, held * N)].astype(F32)
    c_out[...] = c_ref[:, at(g_other, held * N)].astype(F32)
    pl.semaphore_wait(barrier, 3)
    b_copy.start()
    send_x(0)

    @pl.loop(0, count)
    def _(c):
        d_out[:, lanes(c)] = decays(other + c)

    d_copy.start()
    c_copy.start()

    @pl.loop(1, count)
    def _(c):
        send_x(c)

    here = (side, 3 - side)
    there = (1 - side, 2 + side)
    for k in range(2):
        b_slot[here[k]] = b_ref[toks(k), at(g_mine, held * N)].astype(F32).T.astype(BF)
        c_slot[here[k]] = c_ref[toks(k), at(g_mine, held * N)]
        for g in range(groups):
            part = slice(g * N, (g + 1) * N)
            scores[k * groups + g] = lax.dot_general(
                c_ref[toks(k), part], b_ref[toks(k), part], (((1,), (1,)), ((), ())),
                preferred_element_type=F32,
            )

    @pl.loop(0, count)
    def _(c):
        both = decays(mine + c)
        d_slot[here[0], :, lanes(c)] = jnp.broadcast_to(both[0:1], (8, chunk))
        d_slot[here[1], :, lanes(c)] = jnp.broadcast_to(both[4:5], (8, chunk))

    row = lax.broadcasted_iota(jnp.int32, (SPAN, SPAN), 0)
    col = lax.broadcasted_iota(jnp.int32, (SPAN, SPAN), 1)

    def diagonal(unit):
        group = (unit * UNIT) // per_group
        for k in range(2):
            grouped = scores[k * groups + group]
            x = x_ref[toks(k), lanes(unit)]
            parts = []
            for h in range(UNIT):
                down = cols_ref[unit, toks(k), h : h + 1]
                gaps = jnp.where(row >= col, down - rows_ref[unit, h : h + 1, toks(k)], -jnp.inf)
                weights = (grouped * jnp.exp(gaps) * step_ref[unit, h : h + 1, toks(k)]).astype(BF)
                own = x[:, h * width : (h + 1) * width]
                part = jnp.dot(weights, own, preferred_element_type=F32)
                parts.append(part + skip_ref[unit * UNIT + h] * own.astype(F32))
            acc[toks(k), lanes(unit)] = jnp.concatenate(parts, axis=1)

    def finish(unit, k, y):
        scale = spread(jnp.exp(cols_ref[unit, toks(k), 0:UNIT]), width)
        o_ref[toks(k), lanes(unit)] = (acc[toks(k), lanes(unit)] + y * scale).astype(BF)

    @pl.loop(0, count)
    def _(c):
        diagonal(mine + c)

    b_copy.wait_recv()
    d_copy.wait_recv()
    for k in range(2):
        b_slot[there[k]] = b_in[toks(k), :].T.astype(BF)
        d_slot[there[k]] = jnp.broadcast_to(d_in[4 * k : 4 * k + 1, :], d_in.shape)
    c_copy.wait_recv()
    for k in range(2):
        c_slot[there[k]] = c_in[toks(k), :].astype(BF)

    def group_rows(c):
        return at((c * UNIT) // per_group * N, N)

    def outputs(c, k, first, second):
        early = jnp.dot(c_slot[2 * k, :, group_rows(c)], first.astype(BF), preferred_element_type=F32)
        late = jnp.dot(
            c_slot[2 * k + 1, :, group_rows(c)], second.astype(BF), preferred_element_type=F32
        )
        is_early = here[k] == 2 * k
        y_out[k, c] = jnp.where(is_early, late, early)
        y_copy(c, k).start()
        finish(mine + c, k, jnp.where(is_early, early, late))

    def advance(c, slot, entering):
        return d_slot[slot, 0:1, lanes(c)] * entering + states[c, slot]

    def forward(c):
        own = weighted(mine + c)
        for k in range(2):
            states[c, here[k]] = jnp.dot(
                b_slot[here[k], group_rows(c), :], own[toks(k)], preferred_element_type=F32
            )
        x_copy(c).wait_recv()
        for k in range(2):
            states[c, there[k]] = jnp.dot(
                b_slot[there[k], group_rows(c), :], x_in[c, toks(k), :].astype(BF),
                preferred_element_type=F32,
            )

        @pl.when(level == 0)
        def _():
            f_in[c] = jnp.zeros(f_in.shape[1:], F32)

        @pl.when(level > 0)
        def _():
            f_copy(c).wait_recv()

        first = f_in[c]
        second = advance(c, 0, first)
        last = advance(c, 1, second)

        @pl.when(level < levels - 1)
        def _():
            f_out[c] = last
            f_copy(c).start()

        @pl.when(level == levels - 1)
        def _():
            k_in[c] = last

        outputs(c, 0, first, second)

    def backward(c):
        @pl.when(level < levels - 1)
        def _():
            k_copy(c).wait_recv()

        first = k_in[c]
        second = advance(c, 2, first)

        @pl.when(level > 0)
        def _():
            k_out[c] = advance(c, 3, second)
            k_copy(c).start()

        outputs(c, 1, first, second)

    lag = 2 * (levels - level) - 1

    @pl.loop(0, count + 2 * levels - 1 + REST)
    def _(t):
        @pl.when(t < count)
        def _():
            forward(t)

        @pl.when(jnp.logical_and(t >= lag, t < lag + count))
        def _():
            backward(t - lag)

        @pl.when(t < count)
        def _():
            diagonal(other + t)

        @pl.when(jnp.logical_and(t >= lag + REST, t < lag + REST + count))
        def _():
            c = t - lag - REST
            for k in range(2):
                y_copy(c, k).wait_recv()
                finish(other + c, k, y_in[k, c])

    for copy in (b_copy, c_copy, d_copy):
        copy.wait_send()

    @pl.loop(0, count)
    def _(c):
        x_copy(c).wait_send()

        @pl.when(level < levels - 1)
        def _():
            f_copy(c).wait_send()

        @pl.when(level > 0)
        def _():
            k_copy(c).wait_send()

        for k in range(2):
            y_copy(c, k).wait_send()


def on_device(features, log_decay, step_size, b_matrix, c_matrix, skip_gain):
    heads, rows = log_decay.shape
    lanes = features.shape[1]
    width = lanes // heads
    groups = b_matrix.shape[1] // N
    per_group = heads // groups
    units = heads // UNIT
    n = lax.axis_size("ctx")

    upto = (jnp.arange(SPAN)[:, None] <= jnp.arange(SPAN)[None, :]).astype(F32)
    cumulative = jnp.einsum(
        "hks,st->hkt", log_decay.reshape(heads, 2, SPAN), upto, precision=lax.Precision.HIGHEST
    )
    ends = cumulative[:, :, -1]
    coeffs = jnp.exp(ends[:, :, None] - cumulative).reshape(heads, rows) * step_size
    cum_rows = cumulative.reshape(units, UNIT, rows)
    step_rows = step_size.reshape(units, UNIT, rows)
    columns = jnp.concatenate([cum_rows, coeffs.reshape(units, UNIT, rows)], axis=1)
    columns = jnp.swapaxes(columns, 1, 2)

    half = lanes // 2
    chunk = UNIT * width
    count = half // chunk
    held = max(1, groups // 2)
    vmem = pl.BlockSpec(memory_space=pltpu.VMEM)
    smem = pl.BlockSpec(memory_space=pltpu.SMEM)
    dma = lambda k: pltpu.SemaphoreType.DMA((k,))
    wide = pltpu.VMEM((rows, held * N), F32)
    line = pltpu.VMEM((8, half), F32)
    block = pltpu.VMEM((count, rows, chunk), F32)
    state = pltpu.VMEM((count, N, chunk), F32)
    part = pltpu.VMEM((2, count, SPAN, chunk), F32)
    return pl.pallas_call(
        functools.partial(layer_kernel, n, per_group, width),
        out_shape=jax.ShapeDtypeStruct((rows, lanes), BF),
        in_specs=[vmem] * 6 + [smem],
        out_specs=vmem,
        scratch_shapes=[
            wide, wide, line, block,
            wide, wide, line, block,
            pltpu.VMEM((4, held * N, SPAN), BF),
            pltpu.VMEM((4, SPAN, held * N), BF),
            pltpu.VMEM((4, 8, half), F32),
            pltpu.VMEM((2 * groups, SPAN, SPAN), F32),
            pltpu.VMEM((rows, lanes), F32),
            pltpu.VMEM((count, 4, N, chunk), F32),
            state, state, state, state,
            part, part,
            dma(3), dma(3),
        ] + [dma(count)] * 10,
        compiler_params=pltpu.CompilerParams(
            collective_id=0, has_side_effects=True, vmem_limit_bytes=LIMIT
        ),
    )(features, columns, cum_rows, step_rows, b_matrix, c_matrix, skip_gain)


def solution(mesh):
    placed = (
        P("ctx", "head"),
        P("head", "ctx"),
        P("head", "ctx"),
        P("ctx", "head"),
        P("ctx", "head"),
        P("head"),
    )
    return jax.shard_map(
        on_device, mesh=mesh, in_specs=placed, out_specs=P("ctx", "head"), check_vma=False
    )
```

```python
import functools

import jax
import jax.numpy as jnp
from jax import lax
from jax.experimental import pallas as pl
from jax.experimental.pallas import tpu as pltpu
from jax.sharding import PartitionSpec as P

N = 256
SPAN = 128
UNIT = 4
REST = 3
MESH = pl.DeviceIdType.MESH
LIMIT = 56 * 1024 * 1024
BF = jnp.bfloat16
F32 = jnp.float32


def spread(values, width):
    rows = values.shape[0]
    return jnp.concatenate(
        [jnp.broadcast_to(values[:, h : h + 1], (rows, width)) for h in range(UNIT)], axis=1
    )


def layer_kernel(
    n, per_group, width, x_ref, decay_ref, step_ref, b_ref, c_ref, skip_ref, o_ref, cols_ref, rows_ref,
    b_out, c_out, d_out, x_out, b_in, c_in, d_in, x_in, b_slot, c_slot, d_slot, scores, acc,
    states, f_out, f_in, k_out, k_in, y_out, y_in,
    small_s, small_r, xf_s, xf_r, xk_s, xk_r, f_s, f_r, k_s, k_r, yf_s, yf_r, yk_s, yk_r,
):
    me = lax.axis_index("ctx")
    level, side = me // 2, lax.rem(me, 2)
    levels = n // 2
    partner = me + 1 - 2 * side
    after, before = lax.rem(me + 2, n), lax.rem(me + n - 2, n)
    chunk = UNIT * width
    count = d_in.shape[1] // chunk
    groups = b_ref.shape[1] // N
    held = b_in.shape[1] // N
    mine, other = side * count, (1 - side) * count
    g_mine, g_other = (side * groups) // 2 * N, ((1 - side) * groups) // 2 * N

    def remote(src, dst, send, recv, device):
        return pltpu.make_async_remote_copy(
            src_ref=src, dst_ref=dst, send_sem=send, recv_sem=recv,
            device_id={"ctx": device}, device_id_type=MESH,
        )

    def at(start, length):
        return pl.ds(pl.multiple_of(start, 128), length)

    def lanes(unit):
        return at(unit * chunk, chunk)

    def toks(k):
        return slice(k * SPAN, (k + 1) * SPAN)

    b_copy = remote(b_out, b_in, small_s.at[0], small_r.at[0], partner)
    c_copy = remote(c_out, c_in, small_s.at[1], small_r.at[1], partner)
    d_copy = remote(d_out, d_in, small_s.at[2], small_r.at[2], partner)

    ends_here = level == 0
    sends_less = jnp.logical_and(ends_here, side == 0)
    gets_less = jnp.logical_and(ends_here, side == 1)

    def x_copy(c, k):
        send, recv = (xf_s, xf_r) if k == 0 else (xk_s, xk_r)
        return remote(x_out.at[k, c], x_in.at[k, c], send.at[c], recv.at[c], partner)

    def f_copy(c):
        return remote(f_out.at[c], f_in.at[c], f_s.at[c], f_r.at[c], after)

    def k_copy(c):
        return remote(k_out.at[c], k_in.at[c], k_s.at[c], k_r.at[c], before)

    def y_copy(c, k):
        send, recv = (yf_s, yf_r) if k == 0 else (yk_s, yk_r)
        return remote(y_out.at[k, c], y_in.at[k, c], send.at[c], recv.at[c], partner)

    def weighted(unit):
        coeffs = spread(cols_ref[unit, :, UNIT : 2 * UNIT], width)
        return (x_ref[:, lanes(unit)].astype(F32) * coeffs).astype(BF)

    def decays(unit):
        ends = [
            jnp.exp(cols_ref[unit, (k + 1) * SPAN - 8 : (k + 1) * SPAN, 0:UNIT])[7:8] for k in range(2)
        ]
        front, back = (jnp.broadcast_to(spread(e, width), (8, chunk)) for e in ends)
        return jnp.where(lax.broadcasted_iota(jnp.int32, (8, chunk), 0) < 4, front, back)

    def send_x(c):
        ready = weighted(other + c).astype(F32)
        x_out[0, c] = ready[toks(0)]
        x_copy(c, 0).start()

        @pl.when(jnp.logical_not(sends_less))
        def _():
            x_out[1, c] = ready[toks(1)]
            x_copy(c, 1).start()

    barrier = pltpu.get_barrier_semaphore()
    for device in (partner, after, before):
        pl.semaphore_signal(barrier, inc=1, device_id={"ctx": device}, device_id_type=MESH)
    row = lax.broadcasted_iota(jnp.int32, (SPAN, SPAN), 0)
    col = lax.broadcasted_iota(jnp.int32, (SPAN, SPAN), 1)
    upto = (row <= col).astype(F32)
    for k in range(2):
        sums = jnp.dot(
            decay_ref[:, toks(k)], upto, precision=lax.Precision.HIGHEST, preferred_element_type=F32
        )
        coeffs = jnp.exp(sums[:, SPAN - 1 :] - sums) * step_ref[:, toks(k)]
        down, scale = sums.T, coeffs.T
        for u in range(cols_ref.shape[0]):
            own = slice(u * UNIT, (u + 1) * UNIT)
            rows_ref[u, :, toks(k)] = jnp.concatenate([sums[own], step_ref[own, toks(k)]], axis=0)
            cols_ref[u, toks(k), :] = jnp.concatenate([down[:, own], scale[:, own]], axis=1)
    b_out[...] = b_ref[:, at(g_other, held * N)].astype(F32)
    c_out[...] = c_ref[:, at(g_other, held * N)].astype(F32)
    pl.semaphore_wait(barrier, 3)
    b_copy.start()
    send_x(0)

    @pl.loop(0, count)
    def _(c):
        d_out[:, lanes(c)] = decays(other + c)

    d_copy.start()
    c_copy.start()

    @pl.loop(1, count)
    def _(c):
        send_x(c)

    here = (side, 3 - side)
    there = (1 - side, 2 + side)
    for k in range(2):
        b_slot[here[k]] = b_ref[toks(k), at(g_mine, held * N)].astype(F32).T.astype(BF)
        c_slot[here[k]] = c_ref[toks(k), at(g_mine, held * N)]
        for g in range(groups):
            part = slice(g * N, (g + 1) * N)
            scores[k * groups + g] = lax.dot_general(
                c_ref[toks(k), part], b_ref[toks(k), part], (((1,), (1,)), ((), ())),
                preferred_element_type=F32,
            )

    @pl.loop(0, count)
    def _(c):
        both = decays(mine + c)
        d_slot[here[0], :, lanes(c)] = jnp.broadcast_to(both[0:1], (8, chunk))
        d_slot[here[1], :, lanes(c)] = jnp.broadcast_to(both[4:5], (8, chunk))

    def diagonal(unit):
        group = (unit * UNIT) // per_group
        for k in range(2):
            grouped = scores[k * groups + group]
            x = x_ref[toks(k), lanes(unit)]
            parts = []
            for h in range(UNIT):
                down = cols_ref[unit, toks(k), h : h + 1]
                gaps = jnp.where(row >= col, down - rows_ref[unit, h : h + 1, toks(k)], -jnp.inf)
                weights = (grouped * jnp.exp(gaps) * rows_ref[unit, UNIT + h : UNIT + h + 1, toks(k)]).astype(BF)
                own = x[:, h * width : (h + 1) * width]
                part = jnp.dot(weights, own, preferred_element_type=F32)
                parts.append(part + skip_ref[unit * UNIT + h] * own.astype(F32))
            acc[toks(k), lanes(unit)] = jnp.concatenate(parts, axis=1)

    def finish(unit, k, y):
        scale = spread(jnp.exp(cols_ref[unit, toks(k), 0:UNIT]), width)
        o_ref[toks(k), lanes(unit)] = (acc[toks(k), lanes(unit)] + y * scale).astype(BF)

    @pl.loop(0, count)
    def _(c):
        diagonal(mine + c)

    b_copy.wait_recv()
    d_copy.wait_recv()
    for k in range(2):
        b_slot[there[k]] = b_in[toks(k), :].T.astype(BF)
        d_slot[there[k]] = jnp.broadcast_to(d_in[4 * k : 4 * k + 1, :], d_in.shape)
    c_copy.wait_recv()
    for k in range(2):
        c_slot[there[k]] = c_in[toks(k), :].astype(BF)

    def group_rows(c):
        return at((c * UNIT) // per_group * N, N)

    def outputs(c, k, first, second):
        early = jnp.dot(c_slot[2 * k, :, group_rows(c)], first.astype(BF), preferred_element_type=F32)
        late = jnp.dot(
            c_slot[2 * k + 1, :, group_rows(c)], second.astype(BF), preferred_element_type=F32
        )
        is_early = here[k] == 2 * k
        y_out[k, c] = jnp.where(is_early, late, early)

        @pl.when(jnp.logical_not(jnp.logical_and(gets_less, k == 0)))
        def _():
            y_copy(c, k).start()

        finish(mine + c, k, jnp.where(is_early, early, late))

    def advance(c, slot, entering):
        return d_slot[slot, 0:1, lanes(c)] * entering + states[c, slot]

    def forward(c):
        own = weighted(mine + c)
        for k in range(2):
            states[c, here[k]] = jnp.dot(
                b_slot[here[k], group_rows(c), :], own[toks(k)], preferred_element_type=F32
            )
        x_copy(c, 0).wait_recv()
        states[c, there[0]] = jnp.dot(
            b_slot[there[0], group_rows(c), :], x_in[0, c].astype(BF), preferred_element_type=F32
        )

        @pl.when(level == 0)
        def _():
            f_in[c] = jnp.zeros(f_in.shape[1:], F32)

        @pl.when(level > 0)
        def _():
            f_copy(c).wait_recv()

        first = f_in[c]
        second = advance(c, 0, first)
        last = advance(c, 1, second)

        @pl.when(level < levels - 1)
        def _():
            f_out[c] = last
            f_copy(c).start()

        @pl.when(level == levels - 1)
        def _():
            k_in[c] = last

        outputs(c, 0, first, second)

        @pl.when(jnp.logical_not(gets_less))
        def _():
            x_copy(c, 1).wait_recv()
            states[c, there[1]] = jnp.dot(
                b_slot[there[1], group_rows(c), :], x_in[1, c].astype(BF), preferred_element_type=F32
            )

    def backward(c):
        @pl.when(level < levels - 1)
        def _():
            k_copy(c).wait_recv()

        first = k_in[c]
        second = advance(c, 2, first)

        @pl.when(level > 0)
        def _():
            k_out[c] = advance(c, 3, second)
            k_copy(c).start()

        outputs(c, 1, first, second)

    lag = 2 * (levels - level) - 1

    @pl.loop(0, count + 2 * levels - 1 + REST)
    def _(t):
        @pl.when(t < count)
        def _():
            forward(t)

        @pl.when(jnp.logical_and(t >= lag, t < lag + count))
        def _():
            backward(t - lag)

        @pl.when(t < count)
        def _():
            diagonal(other + t)

        @pl.when(jnp.logical_and(t >= lag + REST, t < lag + REST + count))
        def _():
            c = t - lag - REST

            @pl.when(sends_less)
            def _():
                y_in[0, c] = jnp.zeros(y_in.shape[2:], F32)

            @pl.when(jnp.logical_not(sends_less))
            def _():
                y_copy(c, 0).wait_recv()

            y_copy(c, 1).wait_recv()
            for k in range(2):
                finish(other + c, k, y_in[k, c])

    for copy in (b_copy, c_copy, d_copy):
        copy.wait_send()

    @pl.loop(0, count)
    def _(c):
        x_copy(c, 0).wait_send()
        y_copy(c, 1).wait_send()

        @pl.when(jnp.logical_not(sends_less))
        def _():
            x_copy(c, 1).wait_send()

        @pl.when(jnp.logical_not(gets_less))
        def _():
            y_copy(c, 0).wait_send()

        @pl.when(level < levels - 1)
        def _():
            f_copy(c).wait_send()

        @pl.when(level > 0)
        def _():
            k_copy(c).wait_send()


def on_device(features, log_decay, step_size, b_matrix, c_matrix, skip_gain):
    heads, rows = log_decay.shape
    lanes = features.shape[1]
    width = lanes // heads
    groups = b_matrix.shape[1] // N
    per_group = heads // groups
    units = heads // UNIT
    n = lax.axis_size("ctx")

    half = lanes // 2
    chunk = UNIT * width
    count = half // chunk
    held = max(1, groups // 2)
    vmem = pl.BlockSpec(memory_space=pltpu.VMEM)
    smem = pl.BlockSpec(memory_space=pltpu.SMEM)
    dma = lambda k: pltpu.SemaphoreType.DMA((k,))
    wide = pltpu.VMEM((rows, held * N), F32)
    line = pltpu.VMEM((8, half), F32)
    state = pltpu.VMEM((count, N, chunk), F32)
    part = pltpu.VMEM((2, count, SPAN, chunk), F32)
    return pl.pallas_call(
        functools.partial(layer_kernel, n, per_group, width),
        out_shape=jax.ShapeDtypeStruct((rows, lanes), BF),
        in_specs=[vmem] * 5 + [smem],
        out_specs=vmem,
        scratch_shapes=[
            pltpu.VMEM((units, rows, 2 * UNIT), F32),
            pltpu.VMEM((units, 2 * UNIT, rows), F32),
            wide, wide, line, part,
            wide, wide, line, part,
            pltpu.VMEM((4, held * N, SPAN), BF),
            pltpu.VMEM((4, SPAN, held * N), BF),
            pltpu.VMEM((4, 8, half), F32),
            pltpu.VMEM((2 * groups, SPAN, SPAN), F32),
            pltpu.VMEM((rows, lanes), F32),
            pltpu.VMEM((count, 4, N, chunk), F32),
            state, state, state, state,
            part, part,
            dma(3), dma(3),
        ] + [dma(count)] * 12,
        compiler_params=pltpu.CompilerParams(
            collective_id=0, has_side_effects=True, vmem_limit_bytes=LIMIT
        ),
    )(features, log_decay, step_size, b_matrix, c_matrix, skip_gain)


def solution(mesh):
    placed = (
        P("ctx", "head"),
        P("head", "ctx"),
        P("head", "ctx"),
        P("ctx", "head"),
        P("ctx", "head"),
        P("head"),
    )
    return jax.shard_map(
        on_device, mesh=mesh, in_specs=placed, out_specs=P("ctx", "head"), check_vma=False
    )
```

```python
import functools

import jax
import jax.numpy as jnp
from jax import lax
from jax.experimental import pallas as pl
from jax.experimental.pallas import tpu as pltpu
from jax.sharding import PartitionSpec as P

N = 256
SPAN = 128
UNIT = 4
REST = 5
MESH = pl.DeviceIdType.MESH
LIMIT = 56 * 1024 * 1024
BF = jnp.bfloat16
F32 = jnp.float32


def spread(values, width):
    rows = values.shape[0]
    return jnp.concatenate(
        [jnp.broadcast_to(values[:, h : h + 1], (rows, width)) for h in range(UNIT)], axis=1
    )


def layer_kernel(
    n, per_group, width, x_ref, decay_ref, step_ref, b_ref, c_ref, skip_ref, o_ref, cols_ref, rows_ref,
    b_out, c_out, d_out, x_out, b_in, c_in, d_in, x_in, b_slot, c_slot, d_slot, scores, acc,
    states, f_out, f_in, k_out, k_in, y_out, y_in,
    small_s, small_r, xf_s, xf_r, xk_s, xk_r, f_s, f_r, k_s, k_r, yf_s, yf_r, yk_s, yk_r,
):
    me = lax.axis_index("ctx")
    level, side = me // 2, lax.rem(me, 2)
    levels = n // 2
    partner = me + 1 - 2 * side
    after, before = lax.rem(me + 2, n), lax.rem(me + n - 2, n)
    chunk = UNIT * width
    count = d_in.shape[1] // chunk
    groups = b_ref.shape[1] // N
    held = b_in.shape[1] // N
    mine, other = side * count, (1 - side) * count
    g_mine, g_other = (side * groups) // 2 * N, ((1 - side) * groups) // 2 * N

    def remote(src, dst, send, recv, device):
        return pltpu.make_async_remote_copy(
            src_ref=src, dst_ref=dst, send_sem=send, recv_sem=recv,
            device_id={"ctx": device}, device_id_type=MESH,
        )

    def at(start, length):
        return pl.ds(pl.multiple_of(start, 128), length)

    def lanes(unit):
        return at(unit * chunk, chunk)

    def toks(k):
        return slice(k * SPAN, (k + 1) * SPAN)

    b_copy = remote(b_out, b_in, small_s.at[0], small_r.at[0], partner)
    c_copy = remote(c_out, c_in, small_s.at[1], small_r.at[1], partner)
    d_copy = remote(d_out, d_in, small_s.at[2], small_r.at[2], partner)

    ends_here = level == 0
    sends_less = jnp.logical_and(ends_here, side == 0)
    gets_less = jnp.logical_and(ends_here, side == 1)

    def x_copy(c, k):
        send, recv = (xf_s, xf_r) if k == 0 else (xk_s, xk_r)
        return remote(x_out.at[k, c], x_in.at[k, c], send.at[c], recv.at[c], partner)

    def f_copy(c):
        return remote(f_out.at[c], f_in.at[c], f_s.at[c], f_r.at[c], after)

    def k_copy(c):
        return remote(k_out.at[c], k_in.at[c], k_s.at[c], k_r.at[c], before)

    def y_copy(c, k):
        send, recv = (yf_s, yf_r) if k == 0 else (yk_s, yk_r)
        return remote(y_out.at[k, c], y_in.at[k, c], send.at[c], recv.at[c], partner)

    def weighted(unit):
        coeffs = spread(cols_ref[unit, :, UNIT : 2 * UNIT], width)
        return (x_ref[:, lanes(unit)].astype(F32) * coeffs).astype(BF)

    def decays(unit):
        ends = [
            jnp.exp(cols_ref[unit, (k + 1) * SPAN - 8 : (k + 1) * SPAN, 0:UNIT])[7:8] for k in range(2)
        ]
        front, back = (jnp.broadcast_to(spread(e, width), (8, chunk)) for e in ends)
        return jnp.where(lax.broadcasted_iota(jnp.int32, (8, chunk), 0) < 4, front, back)

    def send_x(c):
        ready = weighted(other + c).astype(F32)
        x_out[0, c] = ready[toks(0)]
        x_copy(c, 0).start()
        x_out[1, c] = ready[toks(1)]

    barrier = pltpu.get_barrier_semaphore()
    for device in (partner, after, before):
        pl.semaphore_signal(barrier, inc=1, device_id={"ctx": device}, device_id_type=MESH)
    row = lax.broadcasted_iota(jnp.int32, (SPAN, SPAN), 0)
    col = lax.broadcasted_iota(jnp.int32, (SPAN, SPAN), 1)
    upto = (row <= col).astype(F32)
    for k in range(2):
        sums = jnp.dot(
            decay_ref[:, toks(k)], upto, precision=lax.Precision.HIGHEST, preferred_element_type=F32
        )
        coeffs = jnp.exp(sums[:, SPAN - 1 :] - sums) * step_ref[:, toks(k)]
        down, scale = sums.T, coeffs.T
        for u in range(cols_ref.shape[0]):
            own = slice(u * UNIT, (u + 1) * UNIT)
            rows_ref[u, :, toks(k)] = jnp.concatenate([sums[own], step_ref[own, toks(k)]], axis=0)
            cols_ref[u, toks(k), :] = jnp.concatenate([down[:, own], scale[:, own]], axis=1)
    b_out[...] = b_ref[:, at(g_other, held * N)].astype(F32)
    c_out[...] = c_ref[:, at(g_other, held * N)].astype(F32)
    pl.semaphore_wait(barrier, 3)
    b_copy.start()
    send_x(0)

    @pl.loop(0, count)
    def _(c):
        d_out[:, lanes(c)] = decays(other + c)

    d_copy.start()
    c_copy.start()

    @pl.loop(1, count)
    def _(c):
        send_x(c)

    @pl.when(jnp.logical_not(sends_less))
    def _():
        @pl.loop(0, count)
        def _(c):
            x_copy(c, 1).start()

    here = (side, 3 - side)
    there = (1 - side, 2 + side)
    for k in range(2):
        b_slot[here[k]] = b_ref[toks(k), at(g_mine, held * N)].astype(F32).T.astype(BF)
        c_slot[here[k]] = c_ref[toks(k), at(g_mine, held * N)]
        for g in range(groups):
            part = slice(g * N, (g + 1) * N)
            scores[k * groups + g] = lax.dot_general(
                c_ref[toks(k), part], b_ref[toks(k), part], (((1,), (1,)), ((), ())),
                preferred_element_type=F32,
            )

    @pl.loop(0, count)
    def _(c):
        both = decays(mine + c)
        d_slot[here[0], :, lanes(c)] = jnp.broadcast_to(both[0:1], (8, chunk))
        d_slot[here[1], :, lanes(c)] = jnp.broadcast_to(both[4:5], (8, chunk))

    def diagonal(unit):
        group = (unit * UNIT) // per_group
        for k in range(2):
            grouped = scores[k * groups + group]
            x = x_ref[toks(k), lanes(unit)]
            parts = []
            for h in range(UNIT):
                down = cols_ref[unit, toks(k), h : h + 1]
                gaps = jnp.where(row >= col, down - rows_ref[unit, h : h + 1, toks(k)], -jnp.inf)
                weights = (grouped * jnp.exp(gaps) * rows_ref[unit, UNIT + h : UNIT + h + 1, toks(k)]).astype(BF)
                own = x[:, h * width : (h + 1) * width]
                part = jnp.dot(weights, own, preferred_element_type=F32)
                parts.append(part + skip_ref[unit * UNIT + h] * own.astype(F32))
            acc[toks(k), lanes(unit)] = jnp.concatenate(parts, axis=1)

    def finish(unit, k, y):
        scale = spread(jnp.exp(cols_ref[unit, toks(k), 0:UNIT]), width)
        o_ref[toks(k), lanes(unit)] = (acc[toks(k), lanes(unit)] + y * scale).astype(BF)

    @pl.loop(0, count)
    def _(c):
        diagonal(mine + c)

    b_copy.wait_recv()
    d_copy.wait_recv()
    for k in range(2):
        b_slot[there[k]] = b_in[toks(k), :].T.astype(BF)
        d_slot[there[k]] = jnp.broadcast_to(d_in[4 * k : 4 * k + 1, :], d_in.shape)
    c_copy.wait_recv()
    for k in range(2):
        c_slot[there[k]] = c_in[toks(k), :].astype(BF)

    def group_rows(c):
        return at((c * UNIT) // per_group * N, N)

    def outputs(c, k, first, second):
        early = jnp.dot(c_slot[2 * k, :, group_rows(c)], first.astype(BF), preferred_element_type=F32)
        late = jnp.dot(
            c_slot[2 * k + 1, :, group_rows(c)], second.astype(BF), preferred_element_type=F32
        )
        is_early = here[k] == 2 * k
        y_out[k, c] = jnp.where(is_early, late, early)

        @pl.when(jnp.logical_not(jnp.logical_and(gets_less, k == 0)))
        def _():
            y_copy(c, k).start()

        finish(mine + c, k, jnp.where(is_early, early, late))

    def advance(c, slot, entering):
        return d_slot[slot, 0:1, lanes(c)] * entering + states[c, slot]

    def forward(c):
        own = weighted(mine + c)
        for k in range(2):
            states[c, here[k]] = jnp.dot(
                b_slot[here[k], group_rows(c), :], own[toks(k)], preferred_element_type=F32
            )
        x_copy(c, 0).wait_recv()
        states[c, there[0]] = jnp.dot(
            b_slot[there[0], group_rows(c), :], x_in[0, c].astype(BF), preferred_element_type=F32
        )

        @pl.when(level == 0)
        def _():
            f_in[c] = jnp.zeros(f_in.shape[1:], F32)

        @pl.when(level > 0)
        def _():
            f_copy(c).wait_recv()

        first = f_in[c]
        second = advance(c, 0, first)
        last = advance(c, 1, second)

        @pl.when(level < levels - 1)
        def _():
            f_out[c] = last
            f_copy(c).start()

        @pl.when(level == levels - 1)
        def _():
            k_in[c] = last

        outputs(c, 0, first, second)

    def backward(c):
        @pl.when(jnp.logical_not(gets_less))
        def _():
            x_copy(c, 1).wait_recv()
            states[c, there[1]] = jnp.dot(
                b_slot[there[1], group_rows(c), :], x_in[1, c].astype(BF), preferred_element_type=F32
            )

        @pl.when(level < levels - 1)
        def _():
            k_copy(c).wait_recv()

        first = k_in[c]
        second = advance(c, 2, first)

        @pl.when(level > 0)
        def _():
            k_out[c] = advance(c, 3, second)
            k_copy(c).start()

        outputs(c, 1, first, second)

    lag = 2 * (levels - level) - 1

    @pl.loop(0, count + 2 * levels - 1 + REST)
    def _(t):
        @pl.when(t < count)
        def _():
            forward(t)

        @pl.when(jnp.logical_and(t >= lag, t < lag + count))
        def _():
            backward(t - lag)

        @pl.when(t < count)
        def _():
            diagonal(other + t)

        @pl.when(jnp.logical_and(t >= lag + REST, t < lag + REST + count))
        def _():
            c = t - lag - REST

            @pl.when(sends_less)
            def _():
                y_in[0, c] = jnp.zeros(y_in.shape[2:], F32)

            @pl.when(jnp.logical_not(sends_less))
            def _():
                y_copy(c, 0).wait_recv()

            y_copy(c, 1).wait_recv()
            for k in range(2):
                finish(other + c, k, y_in[k, c])

    for copy in (b_copy, c_copy, d_copy):
        copy.wait_send()

    @pl.loop(0, count)
    def _(c):
        x_copy(c, 0).wait_send()
        y_copy(c, 1).wait_send()

        @pl.when(jnp.logical_not(sends_less))
        def _():
            x_copy(c, 1).wait_send()

        @pl.when(jnp.logical_not(gets_less))
        def _():
            y_copy(c, 0).wait_send()

        @pl.when(level < levels - 1)
        def _():
            f_copy(c).wait_send()

        @pl.when(level > 0)
        def _():
            k_copy(c).wait_send()


def on_device(features, log_decay, step_size, b_matrix, c_matrix, skip_gain):
    heads, rows = log_decay.shape
    lanes = features.shape[1]
    width = lanes // heads
    groups = b_matrix.shape[1] // N
    per_group = heads // groups
    units = heads // UNIT
    n = lax.axis_size("ctx")

    half = lanes // 2
    chunk = UNIT * width
    count = half // chunk
    held = max(1, groups // 2)
    vmem = pl.BlockSpec(memory_space=pltpu.VMEM)
    smem = pl.BlockSpec(memory_space=pltpu.SMEM)
    dma = lambda k: pltpu.SemaphoreType.DMA((k,))
    wide = pltpu.VMEM((rows, held * N), F32)
    line = pltpu.VMEM((8, half), F32)
    state = pltpu.VMEM((count, N, chunk), F32)
    part = pltpu.VMEM((2, count, SPAN, chunk), F32)
    return pl.pallas_call(
        functools.partial(layer_kernel, n, per_group, width),
        out_shape=jax.ShapeDtypeStruct((rows, lanes), BF),
        in_specs=[vmem] * 5 + [smem],
        out_specs=vmem,
        scratch_shapes=[
            pltpu.VMEM((units, rows, 2 * UNIT), F32),
            pltpu.VMEM((units, 2 * UNIT, rows), F32),
            wide, wide, line, part,
            wide, wide, line, part,
            pltpu.VMEM((4, held * N, SPAN), BF),
            pltpu.VMEM((4, SPAN, held * N), BF),
            pltpu.VMEM((4, 8, half), F32),
            pltpu.VMEM((2 * groups, SPAN, SPAN), F32),
            pltpu.VMEM((rows, lanes), F32),
            pltpu.VMEM((count, 4, N, chunk), F32),
            state, state, state, state,
            part, part,
            dma(3), dma(3),
        ] + [dma(count)] * 12,
        compiler_params=pltpu.CompilerParams(
            collective_id=0, has_side_effects=True, vmem_limit_bytes=LIMIT
        ),
    )(features, log_decay, step_size, b_matrix, c_matrix, skip_gain)


def solution(mesh):
    placed = (
        P("ctx", "head"),
        P("head", "ctx"),
        P("head", "ctx"),
        P("ctx", "head"),
        P("ctx", "head"),
        P("head"),
    )
    return jax.shard_map(
        on_device, mesh=mesh, in_specs=placed, out_specs=P("ctx", "head"), check_vma=False
    )
```
